32 devices in a mesh: head: 4 (over y, core), tok: 8 (over z, x).
Axes of the slice: x: 2, y: 2, z: 4, core: 2. Of those that a mesh axis runs over, the one named last changes fastest.
Arguments:
- queries: bfloat16 [8192, 4096], P('tok', 'head'), may hold values from -100 to 100
- keys: bfloat16 [8192, 4096], P('tok', 'head'), may hold values from -6 to 6
- values: bfloat16 [8192, 4096], P('tok', 'head'), may hold values from -6 to 6
- step_size: float32 [8192, 8], P('tok', 'head'), may hold values from 0.00012207031 to 0.0012207031
- fast_one: bfloat16 [8, 512, 512], P('head'), may hold values from -0.25 to 0.25
- fast_three: bfloat16 [8, 512, 512], P('head'), may hold values from -0.25 to 0.25
- fast_two: bfloat16 [8, 512, 512], P('head'), may hold values from -0.25 to 0.25
- out_proj: bfloat16 [4096, 4096], P('tok', 'head'), may hold values from -0.09375 to 0.09375
- view_units: int32 [16], replicated, may hold values from 1 to 8, 64 in all
- evening: int32 [8, 8], P('tok'), may hold values from 0 to 7, each once within a row
Outputs:
- evened: bfloat16 [8192, 4096], P('tok', 'head')
The draws below stay inside these ranges and needn't reach their ends.
Inputs may be any that keep to these rules, and one draw needn't show every extreme that they name: `view_units`: the lengths sum to 64; the longest is exactly 8. `evening`: each row is a permutation of the token shards.
All inputs are finite; a program needn't handle non-finite values.
Results may differ from the reference program's by a relative error of at most 0.01.
The reference program's roundings to bfloat16 on the way count: a program that leaves them out, or rounds other values in their place, can miss the bound.
Values may be sent and summed in bfloat16 or wider, within the bound.
A program may use at most 128 MiB of HBM per device.

```python
import math
import jax
import jax.numpy as jnp
import numpy as np
from jax import lax

D = 4096
HEADS = 8
DH = 512
FH = 512
TOK_DEV = 1024
VIEW_UNIT = 128
VIEW_MOST = 8
TOKENS = 8192
NVIEWS = 16
TILE = 128
N_TOK = 8


def draw_pair(key):
    base = jax.random.fold_in(key, 7)
    keys_raw = jnp.clip(jax.random.normal(jax.random.fold_in(base, 1), (TOKENS, D), jnp.float32), -6.0, 6.0)
    query_raw = jnp.clip(2.0 * jax.random.normal(jax.random.fold_in(base, 2), (TOKENS, D), jnp.float32), -12.0, 12.0)
    return (query_raw, keys_raw)


def draw_queries(key, part):
    return draw_pair(key)[0].astype(jnp.bfloat16)


def draw_keys(key, part):
    return draw_pair(key)[1].astype(jnp.bfloat16)


def block_levels(own_key, shape, split, smallest, high):
    factor_of, own = 1.0, jax.random.fold_in(own_key, 6)
    for axis_at, shards_of in split:
        steps = jnp.exp(jax.random.uniform(jax.random.fold_in(own, axis_at), (shards_of,), jnp.float32, smallest / len(split), high / len(split)))
        factor_of = factor_of * jnp.repeat(steps, shape[axis_at] // shards_of).reshape([-1 if axis == axis_at else 1 for axis in range(len(shape))])
    return factor_of


def profile(count, total, reach, skew):
    weights = [(1 << 20) // math.isqrt(grade ** skew) + 1 for grade in range(2, count + 1)]
    spare, given = total - reach - (count - 1), [1] * (count - 1)
    while spare > 0:
        candidates = [i for i in range(count - 1) if given[i] < reach]
        mass, budget = sum([weights[i] for i in candidates]), spare
        for i in candidates:
            addition = min(reach - given[i], max(1, budget * weights[i] // mass), spare)
            given[i] = given[i] + addition
            spare = spare - addition
    return np.array([reach] + given)


def ragged(stream_key, number_of, total, bound, lean):
    if number_of == 2:
        one = jax.random.randint(stream_key, (), max(1, total - bound), min(bound, total - 1) + 1)
        return jnp.stack([one, total - one])
    lengths = jnp.asarray(profile(number_of, total, bound, lean), jnp.int32)
    pairs = (number_of - 1) // 2
    giver, taker = lengths[1:1 + 2 * pairs:2], lengths[2:2 + 2 * pairs:2]
    margin = jnp.minimum(giver - 1, bound - taker)
    moved = jax.random.randint(jax.random.fold_in(stream_key, 1), (pairs,), 0, 1 << 20) % (margin + 1)
    lengths = lengths.at[1:1 + 2 * pairs:2].set(giver - moved).at[2:2 + 2 * pairs:2].set(taker + moved)
    return lengths[jax.random.permutation(jax.random.fold_in(stream_key, 2), number_of)]


def bell_draw(key, extent, deviation, bound, split=(), held_as=jnp.bfloat16):
    array = deviation * jax.random.normal(key, extent, jnp.float32)
    if split:
        array = array * block_levels(key, extent, split, -0.22, 0.18)
    return jnp.clip(array, -bound, bound).astype(held_as)


def setup_inputs(seed: int = 0) -> dict:
    seeds = jax.random.split(jax.random.key(seed), 11)
    return {
        "queries": draw_queries(jax.random.fold_in(seeds[10], 71), 0),
        "keys": draw_keys(jax.random.fold_in(seeds[10], 71), 0),
        "values": bell_draw(seeds[2], (TOKENS, D), 1.0, 6.0, ((0, 8), (1, 4))),
        "step_size": jnp.clip(jnp.exp(math.log(0.0012207031) - 2.3025851 * jax.random.uniform(seeds[3], (TOKENS, HEADS), jnp.float32) ** block_levels(seeds[3], (TOKENS, HEADS), ((0, 8), (1, 4)), -0.2, 0.2)), 0.00012207031, 0.0012207031),
        "fast_one": bell_draw(seeds[4], (HEADS, DH, FH), DH ** -0.5, 0.25, ((0, 4),)),
        "fast_three": bell_draw(seeds[5], (HEADS, DH, FH), DH ** -0.5, 0.25, ((0, 4),)),
        "fast_two": bell_draw(seeds[6], (HEADS, FH, DH), FH ** -0.5, 0.25, ((0, 4),)),
        "out_proj": bell_draw(seeds[7], (D, D), D ** -0.5, 0.09375, ((0, 8), (1, 4))),
        "view_units": ragged(seeds[8], NVIEWS, TOKENS // VIEW_UNIT, VIEW_MOST, 1).astype(jnp.int32),
        "evening": jax.vmap(lambda own: jax.random.permutation(own, N_TOK))(jax.random.split(seeds[9], N_TOK)).reshape((N_TOK, N_TOK)).astype(jnp.int32),
    }


def view_lookup(view_units, positions):
    view_ends = jnp.cumsum(view_units.astype(jnp.int32)).astype(jnp.int32) * VIEW_UNIT
    inside = (positions >= 0) & (positions < TOKENS)
    labels = lax.optimization_barrier(jnp.sum((positions[:, None] >= view_ends[None, :]).astype(jnp.int32), axis=1))
    return jnp.where(inside, labels, -1)

def rms_rows(rows):
    return rows * lax.rsqrt(lax.optimization_barrier(jnp.mean(rows * rows, axis=-1, keepdims=True)) + 1e-06)

def fast_head(operands):
    query_norm, key_norm, value_rows, rates, gate_w, up_w, down_w = operands
    gate_pre = jnp.dot(key_norm, gate_w, preferred_element_type=jnp.float32)
    up_pre = jnp.dot(key_norm, up_w, preferred_element_type=jnp.float32)
    gate_sig = jax.nn.sigmoid(gate_pre)
    hidden_keys = (gate_pre * gate_sig * up_pre).astype(jnp.bfloat16)
    descent = (-rates[:, None] * value_rows.astype(jnp.float32)).astype(jnp.bfloat16)
    grad_two = jnp.dot(hidden_keys.T, descent, preferred_element_type=jnp.float32)
    back = jnp.dot(descent, down_w.T, preferred_element_type=jnp.float32)
    grad_gate = (back * up_pre * gate_sig * (1.0 + gate_pre * (1.0 - gate_sig))).astype(jnp.bfloat16)
    grad_up = (back * gate_pre * gate_sig).astype(jnp.bfloat16)
    grad_one = jnp.dot(key_norm.T, grad_gate, preferred_element_type=jnp.float32)
    grad_three = jnp.dot(key_norm.T, grad_up, preferred_element_type=jnp.float32)
    new_one = (gate_w.astype(jnp.float32) - grad_one).astype(jnp.bfloat16)
    new_three = (up_w.astype(jnp.float32) - grad_three).astype(jnp.bfloat16)
    new_two = (down_w.astype(jnp.float32) - grad_two).astype(jnp.bfloat16)
    gate_q = jnp.dot(query_norm, new_one, preferred_element_type=jnp.float32)
    up_q = jnp.dot(query_norm, new_three, preferred_element_type=jnp.float32)
    hidden_q = (gate_q * jax.nn.sigmoid(gate_q) * up_q).astype(jnp.bfloat16)
    return jnp.dot(hidden_q, new_two, preferred_element_type=jnp.float32)

def reference(queries, keys, values, step_size, fast_one, fast_three, fast_two, out_proj, view_units, evening):
    scale = DH ** (-0.5)
    query_block = min(512, TOK_DEV)
    half_span = VIEW_MOST * VIEW_UNIT
    span = query_block + 2 * half_span
    key_pad = jnp.pad(keys, ((half_span, half_span), (0, 0)))
    value_pad = jnp.pad(values, ((half_span, half_span), (0, 0)))
    all_labels = view_lookup(view_units, jnp.arange(TOKENS + 2 * half_span, dtype=jnp.int32) - half_span)

    def attend(block_index):
        start = (block_index * query_block).astype(jnp.int32)
        query_rows = lax.dynamic_slice_in_dim(queries, start, query_block, 0).reshape(query_block, HEADS, DH)
        key_rows = lax.dynamic_slice_in_dim(key_pad, start, span, 0).reshape(span, HEADS, DH)
        value_rows = lax.dynamic_slice_in_dim(value_pad, start, span, 0).reshape(span, HEADS, DH)
        query_views = lax.dynamic_slice_in_dim(all_labels, start + half_span, query_block, 0)
        key_views = lax.dynamic_slice_in_dim(all_labels, start, span, 0)
        scores = jnp.einsum('qhd,khd->hqk', query_rows.astype(jnp.float32), key_rows.astype(jnp.float32)) * scale
        same_view = query_views[:, None] == key_views[None, :]
        scores = jnp.where(same_view[None], scores, -1e+30)
        top = lax.optimization_barrier(jnp.max(scores, axis=-1, keepdims=True))
        weights = jnp.exp(scores - top)
        probs = (weights / lax.optimization_barrier(jnp.sum(weights, axis=-1, keepdims=True))).astype(jnp.bfloat16)
        out_rows = jnp.einsum('hqk,khd->qhd', probs.astype(jnp.float32), value_rows.astype(jnp.float32))
        return out_rows.reshape(query_block, D)
    attended = lax.map(attend, jnp.arange(TOKENS // query_block, dtype=jnp.int32)).reshape(TOKENS, D)
    query_norm = rms_rows(queries.astype(jnp.float32).reshape(TOKENS, HEADS, DH)).astype(jnp.bfloat16)
    key_norm = rms_rows(keys.astype(jnp.float32).reshape(TOKENS, HEADS, DH)).astype(jnp.bfloat16)
    operands = (query_norm.transpose(1, 0, 2), key_norm.transpose(1, 0, 2), values.reshape(TOKENS, HEADS, DH).transpose(1, 0, 2), step_size.T, fast_one, fast_three, fast_two)
    fast_out = lax.map(fast_head, operands).transpose(1, 0, 2).reshape(TOKENS, D)
    mixed = (attended + fast_out).astype(jnp.bfloat16)
    projected = jnp.dot(mixed, out_proj, preferred_element_type=jnp.float32).astype(jnp.bfloat16)
    tiles = projected.reshape(N_TOK, N_TOK, TILE, D)
    match = (evening[:, :, None] == jnp.arange(N_TOK, dtype=jnp.int32)[None, None, :]).astype(jnp.int32)
    chosen = jnp.argmax(match, axis=1).astype(jnp.int32)
    picked = jnp.take_along_axis(tiles, chosen[:, :, None, None], axis=1)
    return picked.transpose(1, 0, 2, 3).reshape(TOKENS, D)
```

```python
import jax
import jax.numpy as jnp
from jax import lax
from jax.experimental import pallas as pl
from jax.experimental.pallas import tpu as pltpu
from jax.sharding import PartitionSpec as P

DH = 512
VIEW_UNIT = 128
VIEW_MOST = 8


def from_behind(value, axis, steps):
    count = lax.axis_size(axis)
    leading, last = (max(0, -steps), min(count, count - steps))
    return lax.ppermute(value, axis, [(source, source + steps) for source in range(leading, last)])


def rms_rows(rows):
    return rows * lax.rsqrt(jnp.mean(rows * rows, axis=-1, keepdims=True) + 1e-06)


def attend_kernel(
    first_ref, last_ref, q_ref, kp_ref, ko_ref, kn_ref, vp_ref, vo_ref, vn_ref, o_ref, k_win, v_win
):
    halo, own = kp_ref.shape[0], ko_ref.shape[0]
    unit = pl.program_id(1)

    @pl.when(unit == 0)
    def _():
        k_win[:halo, :] = kp_ref[...]
        k_win[halo : halo + own, :] = ko_ref[...]
        k_win[halo + own :, :] = kn_ref[...]
        v_win[:halo, :] = vp_ref[...]
        v_win[halo : halo + own, :] = vo_ref[...]
        v_win[halo + own :, :] = vn_ref[...]

    span = VIEW_MOST * VIEW_UNIT
    first, last = first_ref[unit], last_ref[unit]
    base = jnp.clip(first, 0, k_win.shape[0] // VIEW_UNIT - VIEW_MOST)
    rows = pl.ds(pl.multiple_of(base * VIEW_UNIT, VIEW_UNIT), span)
    scores = lax.dot_general(
        q_ref[...], k_win[rows, :], (((1,), (1,)), ((), ())), preferred_element_type=jnp.float32
    ) * (DH ** (-0.5))
    column = lax.broadcasted_iota(jnp.int32, scores.shape, 1) + base * VIEW_UNIT
    inside = (column >= first * VIEW_UNIT) & (column < last * VIEW_UNIT)
    scores = jnp.where(inside, scores, -1e30)
    top = jnp.max(scores, axis=-1, keepdims=True)
    weights = jnp.exp(scores - top)
    probs = (weights / jnp.sum(weights, axis=-1, keepdims=True)).astype(jnp.bfloat16)
    o_ref[...] = jnp.dot(probs, v_win[rows, :], preferred_element_type=jnp.float32)


def attention(first, last, queries, k_prev, keys, k_next, v_prev, values, v_next):
    own, width = queries.shape
    halo = k_prev.shape[0]
    heads = width // DH
    part = lambda rows: pl.BlockSpec((rows, DH), lambda h, u, *_: (0, h))
    unit = pl.BlockSpec((VIEW_UNIT, DH), lambda h, u, *_: (u, h))
    return pl.pallas_call(
        attend_kernel,
        grid_spec=pltpu.PrefetchScalarGridSpec(
            num_scalar_prefetch=2,
            grid=(heads, own // VIEW_UNIT),
            in_specs=[unit] + [part(halo), part(own), part(halo)] * 2,
            out_specs=unit,
            scratch_shapes=[pltpu.VMEM((own + 2 * halo, DH), jnp.bfloat16)] * 2,
        ),
        out_shape=jax.ShapeDtypeStruct((own, width), jnp.float32),
        compiler_params=pltpu.CompilerParams(vmem_limit_bytes=40 * 1024 * 1024),
        cost_estimate=pl.CostEstimate(
            flops=4 * own * width * VIEW_MOST * VIEW_UNIT,
            bytes_accessed=8 * own * width * 2,
            transcendentals=own * heads * VIEW_MOST * VIEW_UNIT,
        ),
    )(first, last, queries, k_prev, keys, k_next, v_prev, values, v_next)


def local(
    queries, keys, values, step_size, fast_one, fast_three, fast_two, out_proj, view_units, evening
):
    shard_count = lax.axis_size("tok")
    my_shard = lax.axis_index("tok")
    tok_dev = queries.shape[0]
    local_width = queries.shape[1]
    heads_here = local_width // DH
    halo = (VIEW_MOST - 1) * VIEW_UNIT
    full_proj = lax.all_gather(out_proj, "tok", axis=0, tiled=True)
    k_prev = from_behind(keys[tok_dev - halo :], "tok", 1)
    k_next = from_behind(keys[:halo], "tok", -1)
    v_prev = from_behind(values[tok_dev - halo :], "tok", 1)
    v_next = from_behind(values[:halo], "tok", -1)
    units_here = tok_dev // VIEW_UNIT
    count = view_units.shape[0]
    before = jnp.arange(count)[:, None] > jnp.arange(count)[None, :]
    starts = jnp.sum(jnp.where(before, view_units[None, :], 0), axis=1)
    ends = starts + view_units
    here = my_shard * units_here + jnp.arange(units_here, dtype=jnp.int32)
    mine = (here[:, None] >= starts[None, :]) & (here[:, None] < ends[None, :])
    shift = halo // VIEW_UNIT - my_shard * units_here
    first = jnp.sum(jnp.where(mine, starts[None, :], 0), axis=1) + shift
    last = jnp.sum(jnp.where(mine, ends[None, :], 0), axis=1) + shift
    query_norm = rms_rows(queries.reshape(tok_dev, heads_here, DH).astype(jnp.float32)).astype(
        jnp.bfloat16
    )
    key_norm = rms_rows(keys.reshape(tok_dev, heads_here, DH).astype(jnp.float32)).astype(
        jnp.bfloat16
    )
    gate_pre = jnp.einsum("thd,hdf->htf", key_norm, fast_one, preferred_element_type=jnp.float32)
    up_pre = jnp.einsum("thd,hdf->htf", key_norm, fast_three, preferred_element_type=jnp.float32)
    gate_sig = jax.nn.sigmoid(gate_pre)
    hidden_keys = (gate_pre * gate_sig * up_pre).astype(jnp.bfloat16)
    descent = (
        -step_size[:, :, None] * values.reshape(tok_dev, heads_here, DH).astype(jnp.float32)
    ).astype(jnp.bfloat16)
    grad_two = jnp.einsum("htf,thd->hfd", hidden_keys, descent, preferred_element_type=jnp.float32)
    back = jnp.einsum("thd,hfd->htf", descent, fast_two, preferred_element_type=jnp.float32)
    grad_gate = (back * up_pre * gate_sig * (1.0 + gate_pre * (1.0 - gate_sig))).astype(
        jnp.bfloat16
    )
    grad_up = (back * gate_pre * gate_sig).astype(jnp.bfloat16)
    grad_one = jnp.einsum("thd,htf->hdf", key_norm, grad_gate, preferred_element_type=jnp.float32)
    grad_three = jnp.einsum("thd,htf->hdf", key_norm, grad_up, preferred_element_type=jnp.float32)
    grads = jnp.stack([grad_one, grad_three, grad_two]).reshape(-1, DH)
    old = jnp.stack([fast_one, fast_three, fast_two]).reshape(-1, DH)
    share = grads.shape[0] // shard_count
    total = lax.psum_scatter(grads, "tok", scatter_dimension=0, tiled=True)
    old_share = lax.dynamic_slice_in_dim(old, my_shard * share, share, 0)
    new_share = (old_share.astype(jnp.float32) - total).astype(jnp.bfloat16)
    new = lax.all_gather(new_share, "tok", axis=0, tiled=True)
    new_one, new_three, new_two = new.reshape((3,) + fast_one.shape)
    gate_q = jnp.einsum("thd,hdf->htf", query_norm, new_one, preferred_element_type=jnp.float32)
    up_q = jnp.einsum("thd,hdf->htf", query_norm, new_three, preferred_element_type=jnp.float32)
    hidden_q = (gate_q * jax.nn.sigmoid(gate_q) * up_q).astype(jnp.bfloat16)
    fast_out = jnp.einsum(
        "htf,hfd->thd", hidden_q, new_two, preferred_element_type=jnp.float32
    ).reshape(tok_dev, local_width)
    attended = attention(first, last, queries, k_prev, keys, k_next, v_prev, values, v_next)
    mixed = (attended + fast_out).astype(jnp.bfloat16)
    tile = tok_dev // shard_count
    targets = evening.reshape(shard_count)
    ids = jnp.arange(shard_count, dtype=jnp.int32)
    order = jnp.sum(jnp.where(targets[None, :] == ids[:, None], ids[None, :], 0), axis=1)
    mixed = jnp.concatenate(
        [lax.dynamic_slice_in_dim(mixed, order[d] * tile, tile, 0) for d in range(shard_count)]
    )
    mixed_full = lax.all_gather(mixed, "head", axis=1, tiled=True)
    outgoing = jnp.dot(mixed_full, full_proj, preferred_element_type=jnp.float32).astype(
        jnp.bfloat16
    )
    return lax.all_to_all(outgoing, "tok", split_axis=0, concat_axis=0, tiled=True)


def solution(mesh):
    return jax.shard_map(
        local,
        mesh=mesh,
        in_specs=(
            P("tok", "head"),
            P("tok", "head"),
            P("tok", "head"),
            P("tok", "head"),
            P("head", None, None),
            P("head", None, None),
            P("head", None, None),
            P("tok", "head"),
            P(),
            P("tok", None),
        ),
        out_specs=P("tok", "head"),
        check_vma=False,
    )
```

```python
import jax
import jax.numpy as jnp
from jax import lax
from jax.experimental import pallas as pl
from jax.experimental.pallas import tpu as pltpu
from jax.sharding import PartitionSpec as P

DH = 512
VIEW_UNIT = 128
VIEW_MOST = 8


def from_behind(value, axis, steps):
    count = lax.axis_size(axis)
    leading, last = (max(0, -steps), min(count, count - steps))
    return lax.ppermute(value, axis, [(source, source + steps) for source in range(leading, last)])


def around(value, axis, steps):
    count = lax.axis_size(axis)
    return lax.ppermute(value, axis, [(at, (at + steps) % count) for at in range(count)])


def by_source(arrived, me):
    count, rows = len(arrived), arrived[0].shape[0]
    twice = jnp.concatenate(arrived[::-1] * 2)
    return lax.dynamic_slice_in_dim(twice, (count - 1 - me) * rows, count * rows, 0)


def rms_rows(rows):
    return rows * lax.rsqrt(jnp.mean(rows * rows, axis=-1, keepdims=True) + 1e-06)


def attend_kernel(
    first_ref, last_ref, q_ref, kp_ref, ko_ref, kn_ref, vp_ref, vo_ref, vn_ref, o_ref, k_win, v_win
):
    halo, own = kp_ref.shape[0], ko_ref.shape[0]
    unit = pl.program_id(1)

    @pl.when(unit == 0)
    def _():
        k_win[:halo, :] = kp_ref[...]
        k_win[halo : halo + own, :] = ko_ref[...]
        k_win[halo + own :, :] = kn_ref[...]
        v_win[:halo, :] = vp_ref[...]
        v_win[halo : halo + own, :] = vo_ref[...]
        v_win[halo + own :, :] = vn_ref[...]

    span = VIEW_MOST * VIEW_UNIT
    first, last = first_ref[unit], last_ref[unit]
    base = jnp.clip(first, 0, k_win.shape[0] // VIEW_UNIT - VIEW_MOST)
    rows = pl.ds(pl.multiple_of(base * VIEW_UNIT, VIEW_UNIT), span)
    scores = lax.dot_general(
        q_ref[...], k_win[rows, :], (((1,), (1,)), ((), ())), preferred_element_type=jnp.float32
    ) * (DH ** (-0.5))
    column = lax.broadcasted_iota(jnp.int32, scores.shape, 1) + base * VIEW_UNIT
    inside = (column >= first * VIEW_UNIT) & (column < last * VIEW_UNIT)
    scores = jnp.where(inside, scores, -1e30)
    top = jnp.max(scores, axis=-1, keepdims=True)
    weights = jnp.exp(scores - top)
    probs = (weights / jnp.sum(weights, axis=-1, keepdims=True)).astype(jnp.bfloat16)
    o_ref[...] = jnp.dot(probs, v_win[rows, :], preferred_element_type=jnp.float32)


def attention(first, last, queries, k_prev, keys, k_next, v_prev, values, v_next):
    own, width = queries.shape
    halo = k_prev.shape[0]
    heads = width // DH
    part = lambda rows: pl.BlockSpec((rows, DH), lambda h, u, *_: (0, h))
    unit = pl.BlockSpec((VIEW_UNIT, DH), lambda h, u, *_: (u, h))
    return pl.pallas_call(
        attend_kernel,
        grid_spec=pltpu.PrefetchScalarGridSpec(
            num_scalar_prefetch=2,
            grid=(heads, own // VIEW_UNIT),
            in_specs=[unit] + [part(halo), part(own), part(halo)] * 2,
            out_specs=unit,
            scratch_shapes=[pltpu.VMEM((own + 2 * halo, DH), jnp.bfloat16)] * 2,
        ),
        out_shape=jax.ShapeDtypeStruct((own, width), jnp.float32),
        compiler_params=pltpu.CompilerParams(vmem_limit_bytes=40 * 1024 * 1024),
        cost_estimate=pl.CostEstimate(
            flops=4 * own * width * VIEW_MOST * VIEW_UNIT,
            bytes_accessed=8 * own * width * 2,
            transcendentals=own * heads * VIEW_MOST * VIEW_UNIT,
        ),
    )(first, last, queries, k_prev, keys, k_next, v_prev, values, v_next)


def local(
    queries, keys, values, step_size, fast_one, fast_three, fast_two, out_proj, view_units, evening
):
    shard_count = lax.axis_size("tok")
    my_shard = lax.axis_index("tok")
    tok_dev = queries.shape[0]
    local_width = queries.shape[1]
    heads_here = local_width // DH
    halo = (VIEW_MOST - 1) * VIEW_UNIT
    full_proj = lax.all_gather(out_proj, "tok", axis=0, tiled=True)
    k_prev = from_behind(keys[tok_dev - halo :], "tok", 1)
    k_next = from_behind(keys[:halo], "tok", -1)
    v_prev = from_behind(values[tok_dev - halo :], "tok", 1)
    v_next = from_behind(values[:halo], "tok", -1)
    units_here = tok_dev // VIEW_UNIT
    count = view_units.shape[0]
    before = jnp.arange(count)[:, None] > jnp.arange(count)[None, :]
    starts = jnp.sum(jnp.where(before, view_units[None, :], 0), axis=1)
    ends = starts + view_units
    here = my_shard * units_here + jnp.arange(units_here, dtype=jnp.int32)
    mine = (here[:, None] >= starts[None, :]) & (here[:, None] < ends[None, :])
    shift = halo // VIEW_UNIT - my_shard * units_here
    first = jnp.sum(jnp.where(mine, starts[None, :], 0), axis=1) + shift
    last = jnp.sum(jnp.where(mine, ends[None, :], 0), axis=1) + shift
    query_norm = rms_rows(queries.reshape(tok_dev, heads_here, DH).astype(jnp.float32)).astype(
        jnp.bfloat16
    )
    key_norm = rms_rows(keys.reshape(tok_dev, heads_here, DH).astype(jnp.float32)).astype(
        jnp.bfloat16
    )
    gate_pre = jnp.einsum("thd,hdf->htf", key_norm, fast_one, preferred_element_type=jnp.float32)
    up_pre = jnp.einsum("thd,hdf->htf", key_norm, fast_three, preferred_element_type=jnp.float32)
    gate_sig = jax.nn.sigmoid(gate_pre)
    hidden_keys = (gate_pre * gate_sig * up_pre).astype(jnp.bfloat16)
    descent = (
        -step_size[:, :, None] * values.reshape(tok_dev, heads_here, DH).astype(jnp.float32)
    ).astype(jnp.bfloat16)
    grad_two = jnp.einsum("htf,thd->hfd", hidden_keys, descent, preferred_element_type=jnp.float32)
    back = jnp.einsum("thd,hfd->htf", descent, fast_two, preferred_element_type=jnp.float32)
    grad_gate = (back * up_pre * gate_sig * (1.0 + gate_pre * (1.0 - gate_sig))).astype(
        jnp.bfloat16
    )
    grad_up = (back * gate_pre * gate_sig).astype(jnp.bfloat16)
    grad_one = jnp.einsum("thd,htf->hdf", key_norm, grad_gate, preferred_element_type=jnp.float32)
    grad_three = jnp.einsum("thd,htf->hdf", key_norm, grad_up, preferred_element_type=jnp.float32)
    grads = jnp.stack([grad_one, grad_three, grad_two]).reshape(-1, DH)
    old = jnp.stack([fast_one, fast_three, fast_two]).reshape(-1, DH)
    share = grads.shape[0] // shard_count
    block = lambda d: lax.dynamic_slice_in_dim(grads, (d % shard_count) * share, share, 0)
    pieces = [
        around(block(my_shard + r).astype(jnp.bfloat16), "tok", r) for r in range(1, shard_count)
    ]
    pieces, k_prev, k_next = lax.optimization_barrier((pieces, k_prev, k_next))
    total = block(my_shard)
    for piece in pieces:
        total = total + piece.astype(jnp.float32)
    old_share = lax.dynamic_slice_in_dim(old, my_shard * share, share, 0)
    new_share = (old_share.astype(jnp.float32) - total).astype(jnp.bfloat16)
    shares = [new_share] + [around(new_share, "tok", r) for r in range(1, shard_count)]
    shares, v_prev, v_next, full_proj = lax.optimization_barrier(
        (shares, v_prev, v_next, full_proj)
    )
    new = by_source(shares, my_shard)
    new_one, new_three, new_two = new.reshape((3,) + fast_one.shape)
    gate_q = jnp.einsum("thd,hdf->htf", query_norm, new_one, preferred_element_type=jnp.float32)
    up_q = jnp.einsum("thd,hdf->htf", query_norm, new_three, preferred_element_type=jnp.float32)
    hidden_q = (gate_q * jax.nn.sigmoid(gate_q) * up_q).astype(jnp.bfloat16)
    fast_out = jnp.einsum(
        "htf,hfd->thd", hidden_q, new_two, preferred_element_type=jnp.float32
    ).reshape(tok_dev, local_width)
    attended = attention(first, last, queries, k_prev, keys, k_next, v_prev, values, v_next)
    mixed = (attended + fast_out).astype(jnp.bfloat16)
    tile = tok_dev // shard_count
    targets = evening.reshape(shard_count)
    ids = jnp.arange(shard_count, dtype=jnp.int32)
    order = jnp.sum(jnp.where(targets[None, :] == ids[:, None], ids[None, :], 0), axis=1)
    steps = list(range(1, shard_count)) + [0]
    half = shard_count // 2
    arrived = {}
    for group in (steps[:half], steps[half:]):
        tiles = []
        for r in group:
            target = (my_shard + r) % shard_count
            at = jnp.sum(jnp.where(ids == target, order, 0))
            tiles.append(lax.dynamic_slice_in_dim(mixed, at * tile, tile, 0))
        rows = lax.all_gather(jnp.concatenate(tiles), "head", axis=1, tiled=True)
        out = jnp.dot(rows, full_proj, preferred_element_type=jnp.float32).astype(jnp.bfloat16)
        for i, r in enumerate(group):
            piece = out[i * tile : (i + 1) * tile]
            arrived[r] = around(piece, "tok", r) if r else piece
    return by_source([arrived[r] for r in range(shard_count)], my_shard)


def solution(mesh):
    return jax.shard_map(
        local,
        mesh=mesh,
        in_specs=(
            P("tok", "head"),
            P("tok", "head"),
            P("tok", "head"),
            P("tok", "head"),
            P("head", None, None),
            P("head", None, None),
            P("head", None, None),
            P("tok", "head"),
            P(),
            P("tok", None),
        ),
        out_specs=P("tok", "head"),
        check_vma=False,
    )
```

```python
import jax
import jax.numpy as jnp
from jax import lax
from jax.experimental import pallas as pl
from jax.experimental.pallas import tpu as pltpu
from jax.sharding import PartitionSpec as P

DH = 512
VIEW_UNIT = 128
VIEW_MOST = 8


def from_behind(value, axis, steps):
    count = lax.axis_size(axis)
    leading, last = (max(0, -steps), min(count, count - steps))
    return lax.ppermute(value, axis, [(source, source + steps) for source in range(leading, last)])


def around(value, axis, steps):
    count = lax.axis_size(axis)
    return lax.ppermute(value, axis, [(at, (at + steps) % count) for at in range(count)])


def by_source(arrived, me):
    count, rows = len(arrived), arrived[0].shape[0]
    twice = jnp.concatenate(arrived[::-1] * 2)
    return lax.dynamic_slice_in_dim(twice, (count - 1 - me) * rows, count * rows, 0)


def rms_rows(rows):
    return rows * lax.rsqrt(jnp.mean(rows * rows, axis=-1, keepdims=True) + 1e-06)


def attend_kernel(
    first_ref, last_ref, q_ref, kp_ref, ko_ref, kn_ref, vp_ref, vo_ref, vn_ref, o_ref, k_win, v_win
):
    halo, own = kp_ref.shape[0], ko_ref.shape[0]
    unit = pl.program_id(1)

    @pl.when(unit == 0)
    def _():
        k_win[:halo, :] = kp_ref[...]
        k_win[halo : halo + own, :] = ko_ref[...]
        k_win[halo + own :, :] = kn_ref[...]
        v_win[:halo, :] = vp_ref[...]
        v_win[halo : halo + own, :] = vo_ref[...]
        v_win[halo + own :, :] = vn_ref[...]

    span = VIEW_MOST * VIEW_UNIT
    first, last = first_ref[unit], last_ref[unit]
    base = jnp.clip(first, 0, k_win.shape[0] // VIEW_UNIT - VIEW_MOST)
    rows = pl.ds(pl.multiple_of(base * VIEW_UNIT, VIEW_UNIT), span)
    scores = lax.dot_general(
        q_ref[...], k_win[rows, :], (((1,), (1,)), ((), ())), preferred_element_type=jnp.float32
    ) * (DH ** (-0.5))
    column = lax.broadcasted_iota(jnp.int32, scores.shape, 1) + base * VIEW_UNIT
    inside = (column >= first * VIEW_UNIT) & (column < last * VIEW_UNIT)
    scores = jnp.where(inside, scores, -1e30)
    top = jnp.max(scores, axis=-1, keepdims=True)
    weights = jnp.exp(scores - top)
    probs = (weights / jnp.sum(weights, axis=-1, keepdims=True)).astype(jnp.bfloat16)
    o_ref[...] = jnp.dot(probs, v_win[rows, :], preferred_element_type=jnp.float32)


def attention(first, last, queries, k_prev, keys, k_next, v_prev, values, v_next):
    own, width = queries.shape
    halo = k_prev.shape[0]
    heads = width // DH
    part = lambda rows: pl.BlockSpec((rows, DH), lambda h, u, *_: (0, h))
    unit = pl.BlockSpec((VIEW_UNIT, DH), lambda h, u, *_: (u, h))
    return pl.pallas_call(
        attend_kernel,
        grid_spec=pltpu.PrefetchScalarGridSpec(
            num_scalar_prefetch=2,
            grid=(heads, own // VIEW_UNIT),
            in_specs=[unit] + [part(halo), part(own), part(halo)] * 2,
            out_specs=unit,
            scratch_shapes=[pltpu.VMEM((own + 2 * halo, DH), jnp.bfloat16)] * 2,
        ),
        out_shape=jax.ShapeDtypeStruct((own, width), jnp.float32),
        compiler_params=pltpu.CompilerParams(vmem_limit_bytes=40 * 1024 * 1024),
        cost_estimate=pl.CostEstimate(
            flops=4 * own * width * VIEW_MOST * VIEW_UNIT,
            bytes_accessed=8 * own * width * 2,
            transcendentals=own * heads * VIEW_MOST * VIEW_UNIT,
        ),
    )(first, last, queries, k_prev, keys, k_next, v_prev, values, v_next)


def local(
    queries, keys, values, step_size, fast_one, fast_three, fast_two, out_proj, view_units, evening
):
    shard_count = lax.axis_size("tok")
    my_shard = lax.axis_index("tok")
    tok_dev = queries.shape[0]
    local_width = queries.shape[1]
    heads_here = local_width // DH
    halo = (VIEW_MOST - 1) * VIEW_UNIT
    full_proj = lax.all_gather(out_proj, "tok", axis=0, tiled=True)
    k_prev = from_behind(keys[tok_dev - halo :], "tok", 1)
    k_next = from_behind(keys[:halo], "tok", -1)
    v_prev = from_behind(values[tok_dev - halo :], "tok", 1)
    v_next = from_behind(values[:halo], "tok", -1)
    units_here = tok_dev // VIEW_UNIT
    count = view_units.shape[0]
    before = jnp.arange(count)[:, None] > jnp.arange(count)[None, :]
    starts = jnp.sum(jnp.where(before, view_units[None, :], 0), axis=1)
    ends = starts + view_units
    here = my_shard * units_here + jnp.arange(units_here, dtype=jnp.int32)
    mine = (here[:, None] >= starts[None, :]) & (here[:, None] < ends[None, :])
    shift = halo // VIEW_UNIT - my_shard * units_here
    first = jnp.sum(jnp.where(mine, starts[None, :], 0), axis=1) + shift
    last = jnp.sum(jnp.where(mine, ends[None, :], 0), axis=1) + shift
    query_norm = rms_rows(queries.reshape(tok_dev, heads_here, DH).astype(jnp.float32)).astype(
        jnp.bfloat16
    )
    key_norm = rms_rows(keys.reshape(tok_dev, heads_here, DH).astype(jnp.float32)).astype(
        jnp.bfloat16
    )
    gate_pre = jnp.einsum("thd,hdf->htf", key_norm, fast_one, preferred_element_type=jnp.float32)
    up_pre = jnp.einsum("thd,hdf->htf", key_norm, fast_three, preferred_element_type=jnp.float32)
    gate_sig = jax.nn.sigmoid(gate_pre)
    hidden_keys = (gate_pre * gate_sig * up_pre).astype(jnp.bfloat16)
    descent = (
        -step_size[:, :, None] * values.reshape(tok_dev, heads_here, DH).astype(jnp.float32)
    ).astype(jnp.bfloat16)
    grad_two = jnp.einsum("htf,thd->hfd", hidden_keys, descent, preferred_element_type=jnp.float32)
    back = jnp.einsum("thd,hfd->htf", descent, fast_two, preferred_element_type=jnp.float32)
    grad_gate = (back * up_pre * gate_sig * (1.0 + gate_pre * (1.0 - gate_sig))).astype(
        jnp.bfloat16
    )
    grad_up = (back * gate_pre * gate_sig).astype(jnp.bfloat16)
    grad_one = jnp.einsum("thd,htf->hdf", key_norm, grad_gate, preferred_element_type=jnp.float32)
    grad_three = jnp.einsum("thd,htf->hdf", key_norm, grad_up, preferred_element_type=jnp.float32)
    grads = jnp.stack([grad_one, grad_three, grad_two]).reshape(-1, DH)
    old = jnp.stack([fast_one, fast_three, fast_two]).reshape(-1, DH)
    share = grads.shape[0] // shard_count
    block = lambda d: lax.dynamic_slice_in_dim(grads, (d % shard_count) * share, share, 0)
    pieces = [
        around(block(my_shard + r).astype(jnp.bfloat16), "tok", r) for r in range(1, shard_count)
    ]
    pieces, k_prev, k_next = lax.optimization_barrier((pieces, k_prev, k_next))
    total = block(my_shard)
    for piece in pieces:
        total = total + piece.astype(jnp.float32)
    old_share = lax.dynamic_slice_in_dim(old, my_shard * share, share, 0)
    new_share = (old_share.astype(jnp.float32) - total).astype(jnp.bfloat16)
    shares = [new_share] + [around(new_share, "tok", r) for r in range(1, shard_count)]
    shares, v_prev, v_next, full_proj = lax.optimization_barrier(
        (shares, v_prev, v_next, full_proj)
    )
    new = by_source(shares, my_shard)
    new_one, new_three, new_two = new.reshape((3,) + fast_one.shape)
    gate_q = jnp.einsum("thd,hdf->htf", query_norm, new_one, preferred_element_type=jnp.float32)
    up_q = jnp.einsum("thd,hdf->htf", query_norm, new_three, preferred_element_type=jnp.float32)
    hidden_q = (gate_q * jax.nn.sigmoid(gate_q) * up_q).astype(jnp.bfloat16)
    fast_out = jnp.einsum(
        "htf,hfd->thd", hidden_q, new_two, preferred_element_type=jnp.float32
    ).reshape(tok_dev, local_width)
    attended = attention(first, last, queries, k_prev, keys, k_next, v_prev, values, v_next)
    mixed = (attended + fast_out).astype(jnp.bfloat16)
    tile = tok_dev // shard_count
    targets = evening.reshape(shard_count)
    ids = jnp.arange(shard_count, dtype=jnp.int32)
    order = jnp.sum(jnp.where(targets[None, :] == ids[:, None], ids[None, :], 0), axis=1)
    steps = list(range(1, shard_count)) + [0]
    half = shard_count // 2
    tiles = []
    for r in steps:
        target = (my_shard + r) % shard_count
        at = jnp.sum(jnp.where(ids == target, order, 0))
        tiles.append(lax.dynamic_slice_in_dim(mixed, at * tile, tile, 0))
    rows = lax.all_gather(jnp.concatenate(tiles), "head", axis=1, tiled=True)
    arrived = {}
    for begin in (0, half):
        part = rows[begin * tile : (begin + half) * tile]
        out = jnp.dot(part, full_proj, preferred_element_type=jnp.float32).astype(jnp.bfloat16)
        for i, r in enumerate(steps[begin : begin + half]):
            piece = out[i * tile : (i + 1) * tile]
            arrived[r] = around(piece, "tok", r) if r else piece
    return by_source([arrived[r] for r in range(shard_count)], my_shard)


def solution(mesh):
    return jax.shard_map(
        local,
        mesh=mesh,
        in_specs=(
            P("tok", "head"),
            P("tok", "head"),
            P("tok", "head"),
            P("tok", "head"),
            P("head", None, None),
            P("head", None, None),
            P("head", None, None),
            P("tok", "head"),
            P(),
            P("tok", None),
        ),
        out_specs=P("tok", "head"),
        check_vma=False,
    )
```
